512 devices in a mesh: row: 32 (over z_lo, y, core), col: 16 (over z_hi, x).
Axes of the slice: x: 4, y: 8, z: 8 (z_hi: 4, z_lo: 2; z = z_hi * 2 + z_lo), core: 2. Of those that a mesh axis runs over, the one named last changes fastest.
Arguments:
- anchors: bfloat16 [65536, 128], P(('row', 'col')), may hold values from -0.7 to 0.7, as said below
- positives: bfloat16 [65536, 128], P(('col', 'row')), may hold values from -0.7 to 0.7, as said below
- row_lse: bfloat16 [65536], P(('row', 'col')), may hold values from 10 to 12
- column_logsumexp: bfloat16 [65536], P(('col', 'row')), may hold values from 10 to 12
Outputs:
- anchor_grad: float32 [65536, 128], P(('row', 'col'))
- matched_partner_derivative: float32 [65536, 128], P(('col', 'row'))
The draws below stay inside these ranges and needn't reach their ends.
Inputs may be any that keep to these rules, and one draw needn't show every extreme that they name: `anchors`: fingerprint embeddings of recordings in groups of similar ones; each positive is a perturbed copy of its anchor. `positives`: perturbed copies of the anchors.
All inputs are finite; a program needn't handle non-finite values.
Results may differ from the reference program's by a relative error of at most 0.0045.
Values may be sent and summed in bfloat16 or wider, within the bound.
A program may use at most 64 MiB of HBM per device.

```python
import math
import jax
import jax.numpy as jnp
from jax import lax

WIDTH = 128
PAIRS = 65536
SOUND_GROUPS = 4096


def fingerprints(key):
    labels = jax.random.randint(jax.random.fold_in(key, 101), (PAIRS,), 0, SOUND_GROUPS)

    def noise(subkey, shape):
        gauss = jax.random.truncated_normal(subkey, -4.0, 4.0, shape, jnp.float32)
        return gauss
    centers = noise(jax.random.fold_in(key, 102), (SOUND_GROUPS, WIDTH))
    base = centers[labels] + 0.6 * noise(jax.random.fold_in(key, 103), (PAIRS, WIDTH))
    second_view = base + 0.5 * noise(jax.random.fold_in(key, 104), (PAIRS, WIDTH))
    anchor = jnp.clip(base / math.sqrt(1.36 * WIDTH), -0.7, 0.7)
    positive = jnp.clip(second_view / math.sqrt(1.61 * WIDTH), -0.7, 0.7)
    return (anchor, positive)


def draw_anchors(key, part):
    pair = fingerprints(key)
    return pair[0].astype(jnp.bfloat16)


def draw_positives(key, part):
    pair = fingerprints(key)
    return pair[1].astype(jnp.bfloat16)


def levels(rng, dims, cuts, smallest, high):
    factor_of = 1.0
    for position, shards_of in cuts:
        steps = jax.random.uniform(jax.random.fold_in(jax.random.fold_in(rng, 6), position), (shards_of,), jnp.float32, smallest / len(cuts), high / len(cuts))
        factor_of = factor_of * jnp.repeat(jnp.exp(steps), dims[position] // shards_of).reshape((-1,) + (1,) * (len(dims) - 1 - position))
    return factor_of


def setup_inputs(seed: int = 0) -> dict:
    key_of = jax.random.split(jax.random.key(seed), 5)
    anchors = draw_anchors(jax.random.fold_in(key_of[4], 71), 0)
    positives = draw_positives(jax.random.fold_in(key_of[4], 71), 0)
    row_lse = jnp.clip(10.0 + 2.0 * jax.random.uniform(key_of[2], (PAIRS,), jnp.float32) ** levels(key_of[2], (PAIRS,), ((0, 512),), -0.2, 0.2), 10.0, 12.0).astype(jnp.bfloat16)
    column_logsumexp = jnp.clip(10.0 + 2.0 * jax.random.uniform(key_of[3], (PAIRS,), jnp.float32) ** levels(key_of[3], (PAIRS,), ((0, 512),), -0.2, 0.2), 10.0, 12.0).astype(jnp.bfloat16)
    return dict(anchors=anchors, positives=positives, row_lse=row_lse, column_logsumexp=column_logsumexp)


def reference(anchors, positives, row_lse, column_logsumexp):
    features = anchors.shape[1]
    rows_per_step = min(512, PAIRS)
    block_list = PAIRS // rows_per_step
    target_offset_amount = column_logsumexp.astype(jnp.float32)[None, :]

    def advance(summed, number):
        opening = number * rows_per_step
        anchor_blk = lax.dynamic_slice_in_dim(anchors, opening, rows_per_step, 0)
        lse_blk = lax.dynamic_slice_in_dim(row_lse, opening, rows_per_step, 0).astype(jnp.float32)
        scores = jnp.dot(anchor_blk, positives.T, preferred_element_type=jnp.float32) * 10.0
        soft = (jnp.exp(scores - lse_blk[:, None]) + jnp.exp(scores - target_offset_amount)).astype(jnp.bfloat16)
        own_rows = lax.dynamic_slice_in_dim(positives, opening, rows_per_step, 0).astype(jnp.float32)
        grad_rows = 5.0 * jnp.dot(soft, positives, preferred_element_type=jnp.float32) - 10.0 * own_rows
        summed = summed + jnp.dot(soft.T, anchor_blk, preferred_element_type=jnp.float32)
        return summed, grad_rows

    summed, rows_out = lax.scan(advance, jnp.zeros((PAIRS, features), jnp.float32),
                                jnp.arange(block_list, dtype=jnp.int32))
    anchor_grad = rows_out.reshape(PAIRS, features)
    matched_partner_derivative = 5.0 * summed - 10.0 * anchors.astype(jnp.float32)
    return anchor_grad, matched_partner_derivative
```

```python
import jax
import jax.numpy as jnp
from jax import lax
from jax.experimental import pallas as pl
from jax.experimental.pallas import tpu as pltpu
from jax.sharding import PartitionSpec as P

f32, bf16 = jnp.float32, jnp.bfloat16
MESH = pl.DeviceIdType.MESH
WIDTH = 128
BLOCK = 128
SENT = 144
LOG2E = 1.4426950408889634
SCALE = 10.0 * LOG2E
TOP = 12.0
NUM_Y, NUM_X, NUM_ZH = 8, 4, 4
COLUMNS, ROWS = 32, 16

P_KEYS = [
    (j, dy % NUM_Y, kk) for dy in (0, -1, 1, -2, 2, -3, 3, 4) for j in (0, 1) for kk in (0, 1)
]
A_KEYS = [(dz % NUM_ZH, dx % NUM_X) for dx in (0, -1, 1, 2) for dz in (0, -1, 1, 2)]
P_SLOT = {key: i for i, key in enumerate(P_KEYS)}
A_SLOT = {key: i for i, key in enumerate(A_KEYS)}


def ps(j, dy, kk):
    return P_SLOT[j, dy % NUM_Y, kk]


def as_(dz, dx):
    return A_SLOT[dz % NUM_ZH, dx % NUM_X]


def y_limit(sign, j):
    return 4 if (sign > 0) == (j == 0) else 3


def x_limit(sign, dz):
    return 2 if (sign > 0) == (dz % 2 == 0) else 1


def numbering():
    keys = []
    keys += [("p", i) for i in range(1, COLUMNS)]
    keys += [("a", i) for i in range(1, ROWS)]
    keys += ["pos", "anc"]
    keys += [("core", j, dy) for j in (0, 1) for dy in range(NUM_Y)]
    keys += [
        ("y", s, j, d) for s in (1, -1) for j in (0, 1) for d in range(1, y_limit(s, j) + 1)
    ]
    keys += ["z"]
    keys += [
        ("x", s, dz, d)
        for s in (1, -1)
        for dz in range(NUM_ZH)
        for d in range(1, x_limit(s, dz) + 1)
    ]
    keys += [("zh", 2), ("zh", 1), ("zh", -1)]
    return {key: i for i, key in enumerate(keys)}


SEM = numbering()
SUM_KEYS = [k for k in SEM if k not in ("pos", "anc") and k[0] not in ("p", "a")]
SUM_SLOT = {key: i for i, key in enumerate(SUM_KEYS)}

ROW_TILE, COL_TILE = 4, 16


def kernel(
    a_ref, p_ref, la_ref, lp_ref, da_out, dp_out,
    ab, pb, at, ub, vb, acc_a, acc_p, out_s, in_s, perm, send_sem, recv_sem,
):
    r, c = lax.axis_index("row"), lax.axis_index("col")
    core, y, zl = r % 2, (r // 2) % NUM_Y, r // 16
    x, zh = c % NUM_X, c // NUM_X

    def row_dev(zl_, y_, core_):
        return (zl_ * 16 + y_ * 2 + core_, c)

    def col_dev(zh_, x_):
        return (r, zh_ * NUM_X + x_)

    sibling = row_dev(zl, y, 1 - core)
    z_pair = row_dev(1 - zl, y, core)
    y_dev = {s: row_dev(zl, (y + s + NUM_Y) % NUM_Y, core) for s in (1, -1)}
    x_dev = {s: col_dev(zh, (x + s + NUM_X) % NUM_X) for s in (1, -1)}
    zh_dev = {s: col_dev((zh + s + NUM_ZH) % NUM_ZH, x) for s in (1, -1)}
    q, b = c * COLUMNS + r, r * ROWS + c
    pos_dev = (q // ROWS, q % ROWS)
    anc_dev = (b % COLUMNS, b // COLUMNS)
    moves = q != b

    peers = [sibling, z_pair, *y_dev.values(), *x_dev.values(), *zh_dev.values()]
    barrier = pltpu.get_barrier_semaphore()
    for dev in peers:
        pl.semaphore_signal(barrier, inc=1, device_id=dev, device_id_type=MESH)

    @pl.when(moves)
    def _():
        for dev in (pos_dev, anc_dev):
            pl.semaphore_signal(barrier, inc=1, device_id=dev, device_id_type=MESH)

    ab[0, :BLOCK, :] = a_ref[...]
    pb[0, :BLOCK, :] = p_ref[...]
    ab[0, BLOCK:, :] = jnp.broadcast_to(la_ref[...], (SENT - BLOCK, WIDTH))
    pb[0, BLOCK:, :] = jnp.broadcast_to(lp_ref[...], (SENT - BLOCK, WIDTH))

    pl.semaphore_wait(barrier, len(peers) + 2 * moves.astype(jnp.int32))

    copies = {}

    def send(key, src, dst, dev):
        copy = pltpu.make_async_remote_copy(
            src_ref=src, dst_ref=dst, send_sem=send_sem.at[SEM[key]], recv_sem=recv_sem.at[SEM[key]],
            device_id=dev, device_id_type=MESH,
        )
        copy.start()
        copies[key] = copy

    def send_p(src, dst, dev):
        send(("p", dst), pb.at[src], pb.at[dst], dev)

    def send_a(src, dst, dev):
        send(("a", dst), ab.at[src], ab.at[dst], dev)

    def got(key):
        copies[key].wait_recv()

    def perm_copies():
        return [
            pltpu.make_async_remote_copy(
                src_ref=src, dst_ref=perm.at[i], send_sem=send_sem.at[SEM[key]],
                recv_sem=recv_sem.at[SEM[key]], device_id=dev, device_id_type=MESH,
            )
            for i, (key, src, dev) in enumerate(
                [("pos", pb.at[0, pl.ds(0, BLOCK)], pos_dev), ("anc", ab.at[0, pl.ds(0, BLOCK)], anc_dev)]
            )
        ]

    send_a(as_(0, 0), as_(-1, 0), zh_dev[1])
    send_a(as_(0, 0), as_(1, 0), zh_dev[-1])
    send_p(ps(0, 0, 0), ps(1, 0, 0), z_pair)
    for s in (1, -1):
        send_p(ps(0, 0, 0), ps(0, -s, 0), y_dev[s])
        send_a(as_(0, 0), as_(0, -s), x_dev[s])
    send_p(ps(0, 0, 0), ps(0, 0, 1), sibling)

    def on_a_z(dz):
        got(("a", as_(dz, 0)))
        if dz == -1:
            send_a(as_(-1, 0), as_(2, 0), zh_dev[1])
        for s in (1, -1):
            send_a(as_(dz, 0), as_(dz, -s), x_dev[s])

    def on_a_x(dz, s):
        got(("a", as_(dz, -s)))
        if x_limit(s, dz) == 2:
            send_a(as_(dz, -s), as_(dz, 2), x_dev[s])

    def on_p_z():
        got(("p", ps(1, 0, 0)))
        for s in (1, -1):
            send_p(ps(1, 0, 0), ps(1, -s, 0), y_dev[s])
        send_p(ps(1, 0, 0), ps(1, 0, 1), sibling)

    def on_p_y(j, s, d):
        got(("p", ps(j, -s * d, 0)))
        if d < y_limit(s, j):
            send_p(ps(j, -s * d, 0), ps(j, -s * (d + 1), 0), y_dev[s])
        send_p(ps(j, -s * d, 0), ps(j, -s * d, 1), sibling)

    on_p_z()
    on_a_z(-1)
    on_a_z(1)
    for s in (1, -1):
        on_p_y(0, s, 1)
        on_a_x(0, s)
    for s in (1, -1):
        on_p_y(1, s, 1)
    on_a_z(2)

    @pl.when(moves)
    def _():
        for copy in perm_copies():
            copy.start()

    for s in (1, -1):
        on_a_x(-1, s)
        on_a_x(1, s)
    for s in (1, -1):
        on_p_y(0, s, 2)
        on_p_y(1, s, 2)
    for s in (1, -1):
        on_a_x(2, s)
    for s in (1, -1):
        on_p_y(0, s, 3)
        on_p_y(1, s, 3)
    for dz in range(NUM_ZH):
        got(("a", as_(dz, 2)))
    on_p_y(0, 1, 4)
    on_p_y(1, -1, 4)
    for j, dy, kk in P_KEYS:
        if kk:
            got(("p", ps(j, dy, 1)))

    def prepare_a(i, _):
        block = ab[i, :BLOCK, :].astype(f32)
        rows = pl.ds(pl.multiple_of(i * BLOCK, BLOCK), BLOCK)
        at[:, rows] = block.T.astype(bf16)
        lse = ab[i, BLOCK:, :].astype(f32)[0:1, :]
        ub[rows, :] = jnp.broadcast_to(jnp.exp(TOP - lse), (BLOCK, BLOCK)).T
        return 0

    def prepare_p(i, _):
        lse = pb[i, BLOCK:, :].astype(f32)[0:8, :]
        vb[:, pl.ds(pl.multiple_of(i * BLOCK, BLOCK), BLOCK)] = jnp.exp(TOP - lse)
        return 0

    lax.fori_loop(0, ROWS, prepare_a, 0)
    lax.fori_loop(0, COLUMNS, prepare_p, 0)
    acc_a[...] = jnp.zeros_like(acc_a)
    acc_p[...] = jnp.zeros_like(acc_p)

    rt, ct = ROW_TILE * BLOCK, COL_TILE * BLOCK

    def tile(n, _):
        i, j = n // (COLUMNS // COL_TILE), n % (COLUMNS // COL_TILE)
        rows, cols = pl.ds(pl.multiple_of(i * rt, rt), rt), pl.ds(pl.multiple_of(j * ct, ct), ct)
        a = ab[pl.ds(i * ROW_TILE, ROW_TILE), :BLOCK, :].reshape(rt, WIDTH)
        p = pb[pl.ds(j * COL_TILE, COL_TILE), :BLOCK, :].reshape(ct, WIDTH)
        t = lax.dot_general(a, p, (((1,), (1,)), ((), ())), preferred_element_type=f32)
        weight = jnp.concatenate([ub[rows, :]] * COL_TILE, axis=1) + vb[0:1, cols]
        soft = (jnp.exp2(t * SCALE - TOP * LOG2E) * weight).astype(bf16)
        acc_a[rows, :] += jnp.dot(soft, p, preferred_element_type=f32)
        acc_p[:, cols] += jnp.dot(at[:, rows], soft, preferred_element_type=f32)
        return 0

    lax.fori_loop(0, (ROWS // ROW_TILE) * (COLUMNS // COL_TILE), tile, 0)

    def own_a(dz, dx):
        i = as_(dz, dx)
        return acc_a[i * BLOCK:(i + 1) * BLOCK, :]

    def own_p(j, dy, kk):
        i = ps(j, dy, kk)
        return acc_p[:, i * BLOCK:(i + 1) * BLOCK]

    def send_sum(key, value, dev):
        i = SUM_SLOT[key]
        out_s[i] = value.astype(bf16)
        send(key, out_s.at[i], in_s.at[i], dev)

    def arrived(key):
        got(key)
        return in_s[SUM_SLOT[key]].astype(f32)

    def chip_p(j, dy):
        return own_p(j, dy, 0) + arrived(("core", j, dy % NUM_Y))

    def y_step(s, j, d):
        value = chip_p(j, s * d)
        if d < y_limit(s, j):
            value += arrived(("y", s, j, d + 1))
        send_sum(("y", s, j, d), value, y_dev[s])

    def x_step(s, dz, d):
        value = own_a(dz, s * d)
        if d < x_limit(s, dz):
            value += arrived(("x", s, dz, d + 1))
        send_sum(("x", s, dz, d), value, x_dev[s])

    def x_total(dz):
        return own_a(dz, 0) + arrived(("x", 1, dz, 1)) + arrived(("x", -1, dz, 1))

    for dy in (4, 3, -3, 2, -2, 1, -1, 0):
        for j in (0, 1):
            send_sum(("core", j, dy % NUM_Y), own_p(j, dy, 1), sibling)
    x_step(1, 2, 2)
    x_step(-1, 1, 2)
    x_step(1, 0, 2)
    x_step(-1, 3, 2)
    y_step(1, 0, 4)
    y_step(-1, 1, 4)
    y_step(1, 1, 3)
    y_step(-1, 0, 3)
    for s in (1, -1):
        for dz in (2, 1, 3, 0):
            if x_limit(s, dz) == 1:
                x_step(s, dz, 1)
    y_step(1, 0, 3)
    y_step(-1, 1, 3)
    x_step(1, 2, 1)
    x_step(-1, 1, 1)
    x_step(1, 0, 1)
    x_step(-1, 3, 1)
    for d in (2, 1):
        y_step(1, 1, d)
        y_step(-1, 0, d)
        y_step(1, 0, d)
        y_step(-1, 1, d)
        if d == 2:
            send_sum(("zh", 2), x_total(2), zh_dev[1])
            send_sum(("zh", -1), x_total(-1 % NUM_ZH), zh_dev[-1])
            send_sum(("zh", 1), x_total(1) + arrived(("zh", 2)), zh_dev[1])

    def y_total(j):
        return chip_p(j, 0) + arrived(("y", 1, j, 1)) + arrived(("y", -1, j, 1))

    send_sum("z", y_total(1), z_pair)

    @pl.when(moves)
    def _():
        for copy in perm_copies():
            copy.wait()

    @pl.when(jnp.logical_not(moves))
    def _():
        perm[0] = pb[0, :BLOCK, :]
        perm[1] = ab[0, :BLOCK, :]

    total_a = x_total(0) + arrived(("zh", 1)) + arrived(("zh", -1))
    da_out[...] = 5.0 * total_a - 10.0 * perm[0].astype(f32)
    total_p = y_total(0) + arrived("z")
    dp_out[...] = 5.0 * total_p.T - 10.0 * perm[1].astype(f32)
    for copy in copies.values():
        copy.wait_send()


def on_device(anchors, positives, row_lse, column_logsumexp):
    vmem = pl.BlockSpec(memory_space=pltpu.VMEM)
    block = jax.ShapeDtypeStruct((BLOCK, WIDTH), f32)
    return pl.pallas_call(
        kernel,
        out_shape=(block, block),
        in_specs=[vmem] * 4,
        out_specs=(vmem, vmem),
        scratch_shapes=[
            pltpu.VMEM((ROWS, SENT, WIDTH), bf16),
            pltpu.VMEM((COLUMNS, SENT, WIDTH), bf16),
            pltpu.VMEM((WIDTH, ROWS * BLOCK), bf16),
            pltpu.VMEM((ROWS * BLOCK, BLOCK), f32),
            pltpu.VMEM((8, COLUMNS * BLOCK), f32),
            pltpu.VMEM((ROWS * BLOCK, WIDTH), f32),
            pltpu.VMEM((WIDTH, COLUMNS * BLOCK), f32),
            pltpu.VMEM((len(SUM_KEYS), BLOCK, WIDTH), bf16),
            pltpu.VMEM((len(SUM_KEYS), BLOCK, WIDTH), bf16),
            pltpu.VMEM((2, BLOCK, WIDTH), bf16),
            pltpu.SemaphoreType.DMA((len(SEM),)),
            pltpu.SemaphoreType.DMA((len(SEM),)),
        ],
        compiler_params=pltpu.CompilerParams(
            collective_id=0, has_side_effects=True, vmem_limit_bytes=48 * 2**20
        ),
        name="infonce_backward",
    )(anchors, positives, row_lse.reshape(1, BLOCK), column_logsumexp.reshape(1, BLOCK))


def solution(mesh):
    return jax.shard_map(
        on_device,
        mesh=mesh,
        in_specs=(
            P(("row", "col"), None),
            P(("col", "row"), None),
            P(("row", "col")),
            P(("col", "row")),
        ),
        out_specs=(P(("row", "col"), None), P(("col", "row"), None)),
        check_vma=False,
    )
```

```python
import jax
import jax.numpy as jnp
from jax import lax
from jax.experimental import pallas as pl
from jax.experimental.pallas import tpu as pltpu
from jax.sharding import PartitionSpec as P

f32, bf16 = jnp.float32, jnp.bfloat16
MESH = pl.DeviceIdType.MESH
WIDTH = 128
BLOCK = 128
SENT = 144
LOG2E = 1.4426950408889634
SCALE = 10.0 * LOG2E
TOP = 12.0
NUM_Y, NUM_X, NUM_ZH = 8, 4, 4
COLUMNS, ROWS = 32, 16

P_GROUPS = {
    "home": [(0, 0), (1, 0)],
    "near": [(0, -1), (0, 1)],
    "next": [(0, -2), (0, 2)],
    "pair_near": [(1, -1), (1, 1)],
    "far": [(0, -3), (0, 3), (0, 4)],
    "pair_next": [(1, -2), (1, 2)],
    "pair_far": [(1, -3), (1, 3), (1, 4)],
}
P_KEYS = [(j, dy % NUM_Y, kk) for group in P_GROUPS.values() for j, dy in group for kk in (0, 1)]
A_KEYS = [(dz % NUM_ZH, dx % NUM_X) for dz in (0, -1, 1, 2) for dx in (0, -1, 1, 2)]
P_SLOT = {key: i for i, key in enumerate(P_KEYS)}
A_SLOT = {key: i for i, key in enumerate(A_KEYS)}


def ps(j, dy, kk):
    return P_SLOT[j, dy % NUM_Y, kk]


def as_(dz, dx):
    return A_SLOT[dz % NUM_ZH, dx % NUM_X]


def p_slots(*names):
    slots = [ps(j, dy, kk) for name in names for j, dy in P_GROUPS[name] for kk in (0, 1)]
    assert slots == list(range(slots[0], slots[0] + len(slots)))
    return slots[0], len(slots)


def a_slots(*dzs):
    slots = [as_(dz, dx) for dz in dzs for dx in (0, -1, 1, 2)]
    assert slots == list(range(slots[0], slots[0] + len(slots)))
    return slots[0], len(slots)


def numbering():
    keys = []
    keys += [("p", i) for i in range(1, COLUMNS)]
    keys += [("a", i) for i in range(1, ROWS)]
    keys += [("core", j, dy) for j in (0, 1) for dy in range(NUM_Y)]
    keys += [("y", j, dy) for j in (0, 1) for dy in range(1, NUM_Y)]
    keys += [("z",)]
    keys += [("x", dz, dx) for dz in range(NUM_ZH) for dx in range(1, NUM_X)]
    keys += [("zh", dz) for dz in range(1, NUM_ZH)]
    return {key: i for i, key in enumerate(keys)}


SEM = numbering()
SUM_KEYS = [k for k in SEM if k[0] not in ("p", "a")]
SUM_SLOT = {key: i for i, key in enumerate(SUM_KEYS)}

BARRIER_Y, BARRIER_ZH = (1, 2, 6, 7), (1, 3)


def kernel(
    a_ref, p_ref, la_ref, lp_ref, da_out, dp_out,
    ab, pb, at, ub, vb, acc_a, acc_p, out_s, in_s, send_sem, recv_sem, load_sem,
):
    loads = [
        pltpu.make_async_copy(a_ref, ab.at[0, pl.ds(0, BLOCK)], load_sem.at[0]),
        pltpu.make_async_copy(p_ref, pb.at[0, pl.ds(0, BLOCK)], load_sem.at[1]),
    ]
    for load in loads:
        load.start()

    r, c = lax.axis_index("row"), lax.axis_index("col")
    core, y, zl = r % 2, (r // 2) % NUM_Y, r // 16
    x, zh = c % NUM_X, c // NUM_X

    def row_dev(zl_, y_, core_):
        return (zl_ * 16 + y_ * 2 + core_, c)

    def col_dev(zh_, x_):
        return (r, zh_ * NUM_X + x_)

    sibling = row_dev(zl, y, 1 - core)
    z_pair = row_dev(1 - zl, y, core)
    y_dev = {d: row_dev(zl, (y + d) % NUM_Y, core) for d in range(1, NUM_Y)}
    x_dev = {d: col_dev(zh, (x + d) % NUM_X) for d in range(1, NUM_X)}
    zh_dev = {d: col_dev((zh + d) % NUM_ZH, x) for d in range(1, NUM_ZH)}

    peers = [sibling, z_pair, *x_dev.values()]
    peers += [y_dev[d] for d in BARRIER_Y] + [zh_dev[d] for d in BARRIER_ZH]
    barrier = pltpu.get_barrier_semaphore()
    for dev in peers:
        pl.semaphore_signal(barrier, inc=1, device_id=dev, device_id_type=MESH)
    ab[0, BLOCK:, :] = jnp.broadcast_to(la_ref[...], (SENT - BLOCK, WIDTH))
    pb[0, BLOCK:, :] = jnp.broadcast_to(lp_ref[...], (SENT - BLOCK, WIDTH))
    for load in loads:
        load.wait()
    pl.semaphore_wait(barrier, len(peers))

    copies = {}

    def send(key, src, dst, dev):
        copy = pltpu.make_async_remote_copy(
            src_ref=src, dst_ref=dst, send_sem=send_sem.at[SEM[key]], recv_sem=recv_sem.at[SEM[key]],
            device_id=dev, device_id_type=MESH,
        )
        copy.start()
        copies[key] = copy

    def got(key):
        copies[key].wait_recv()

    def send_p(src, dst, dev):
        send(("p", dst), pb.at[src], pb.at[dst], dev)

    def send_a(src, dst, dev):
        send(("a", dst), ab.at[src], ab.at[dst], dev)

    def got_p(j, dy, kk):
        got(("p", ps(j, dy, kk)))

    def got_a(dz, dx):
        got(("a", as_(dz, dx)))

    def a_along_x(dz):
        for d in (1, -1, 2):
            send_a(as_(dz, 0), as_(dz, -d), x_dev[d % NUM_X])

    def p_along_y(j, ds):
        for d in ds:
            send_p(ps(j, 0, 0), ps(j, -d, 0), y_dev[d % NUM_Y])

    def to_sibling(j, dy):
        send_p(ps(j, dy, 0), ps(j, dy, 1), sibling)

    def onward(j, s):
        got_p(j, -2 * s, 0)
        send_p(ps(j, -2 * s, 0), ps(j, -3 * s, 0), y_dev[s % NUM_Y])
        if (s > 0) == (j == 0):
            send_p(ps(j, -2 * s, 0), ps(j, 4, 0), y_dev[2 * s % NUM_Y])
        to_sibling(j, -2 * s)

    def prepare_a(dz):
        first, count = a_slots(dz)
        for i in range(first, first + count):
            rows = slice(i * BLOCK, (i + 1) * BLOCK)
            at[:, rows] = ab[i, :BLOCK, :].astype(f32).T.astype(bf16)
            lse = ab[i, BLOCK:, :].astype(f32)[0:1, :]
            ub[rows, :] = jnp.broadcast_to(jnp.exp(TOP - lse), (BLOCK, BLOCK)).T

    def prepare_p(name):
        first, count = p_slots(name)
        for i in range(first, first + count):
            lse = pb[i, BLOCK:, :].astype(f32)[0:8, :]
            vb[:, i * BLOCK:(i + 1) * BLOCK] = jnp.exp(TOP - lse)

    touched = set()

    def tile(row_slots, col_slots):
        (r0, nr), (c0, nc) = row_slots, col_slots
        rows, cols = slice(r0 * BLOCK, (r0 + nr) * BLOCK), slice(c0 * BLOCK, (c0 + nc) * BLOCK)
        a = ab[r0:r0 + nr, :BLOCK, :].reshape(nr * BLOCK, WIDTH)
        p = pb[c0:c0 + nc, :BLOCK, :].reshape(nc * BLOCK, WIDTH)
        t = lax.dot_general(a, p, (((1,), (1,)), ((), ())), preferred_element_type=f32)
        weight = jnp.concatenate([ub[rows, :]] * nc, axis=1) + vb[0:1, cols]
        soft = (jnp.exp2(t * SCALE - TOP * LOG2E) * weight).astype(bf16)
        to_rows = jnp.dot(soft, p, preferred_element_type=f32)
        to_cols = jnp.dot(at[:, rows], soft, preferred_element_type=f32)
        row_keys = {("a", i) for i in range(r0, r0 + nr)}
        col_keys = {("p", i) for i in range(c0, c0 + nc)}
        if row_keys <= touched:
            acc_a[rows, :] += to_rows
        else:
            assert not row_keys & touched
            acc_a[rows, :] = to_rows
        if col_keys <= touched:
            acc_p[:, cols] += to_cols
        else:
            assert not col_keys & touched
            acc_p[:, cols] = to_cols
        touched.update(row_keys | col_keys)

    def own_a(dz, dx):
        i = as_(dz, dx)
        return acc_a[i * BLOCK:(i + 1) * BLOCK, :]

    def own_p(j, dy, kk):
        i = ps(j, dy, kk)
        return acc_p[:, i * BLOCK:(i + 1) * BLOCK]

    def send_sum(key, value, dev):
        i = SUM_SLOT[key]
        out_s[i] = value.astype(bf16)
        send(key, out_s.at[i], in_s.at[i], dev)

    def arrived(*key):
        got(key)
        return in_s[SUM_SLOT[key]].astype(f32)

    def core_sums(*names):
        for name in names:
            for j, dy in P_GROUPS[name]:
                send_sum(("core", j, dy % NUM_Y), own_p(j, dy, 1), sibling)

    def chip_sum(j, dy):
        return own_p(j, dy, 0) + arrived("core", j, dy % NUM_Y)

    def y_sums(*names):
        for name in names:
            for j, dy in P_GROUPS[name]:
                send_sum(("y", j, dy % NUM_Y), chip_sum(j, dy), y_dev[dy % NUM_Y])

    def y_total(j):
        total = chip_sum(j, 0)
        for dy in range(1, NUM_Y):
            total += arrived("y", j, dy)
        return total

    def x_sums(dz):
        for dx in (2, 1, -1):
            send_sum(("x", dz % NUM_ZH, dx % NUM_X), own_a(dz, dx), x_dev[dx % NUM_X])

    def x_total(dz):
        total = own_a(dz, 0)
        for dx in range(1, NUM_X):
            total += arrived("x", dz % NUM_ZH, dx)
        return total

    def zh_sum(dz):
        send_sum(("zh", dz % NUM_ZH), x_total(dz), zh_dev[dz % NUM_ZH])

    def diagonal():
        for dz, dx in A_KEYS:
            i = as_(dz, dx)
            other = (zh + dz) % NUM_ZH * NUM_X + (x + dx) % NUM_X
            j, dy, kk = (core + zl) % 2, (other // 2 + NUM_Y - y) % NUM_Y, (other + core) % 2
            place = jnp.where(dy <= 3, 2 * dy, 15 - 2 * dy)
            k = jnp.where(
                place == 0, 2 * j,
                jnp.where(
                    place <= 2, 4 + 8 * j + 2 * (place - 1),
                    jnp.where(place <= 4, 8 + 14 * j + 2 * (place - 3), 16 + 10 * j + 2 * (place - 5)),
                ),
            ) + kk
            rows, cols = slice(i * BLOCK, (i + 1) * BLOCK), pl.ds(pl.multiple_of(k * BLOCK, BLOCK), BLOCK)
            acc_a[rows, :] -= 2.0 * pb[k, :BLOCK, :].astype(f32)
            acc_p[:, cols] -= 2.0 * at[:, rows].astype(f32)

    send_a(as_(0, 0), as_(-1, 0), zh_dev[1])
    send_a(as_(0, 0), as_(1, 0), zh_dev[3])
    send_p(ps(0, 0, 0), ps(1, 0, 0), z_pair)
    p_along_y(0, (1, -1))
    a_along_x(0)
    p_along_y(0, (2, -2))
    to_sibling(0, 0)

    got_p(1, 0, 0)
    p_along_y(1, (1, -1, 2, -2))
    to_sibling(1, 0)
    for s in (1, -1):
        got_p(0, s, 0)
        to_sibling(0, s)
    got_a(-1, 0)
    send_a(as_(-1, 0), as_(2, 0), zh_dev[1])
    a_along_x(-1)
    got_a(1, 0)
    a_along_x(1)
    for d in (1, -1, 2):
        got_a(0, d)
    prepare_a(0)
    for s in (1, -1):
        got_p(0, s, 1)
    prepare_p("near")
    tile(a_slots(0), p_slots("near"))

    onward(0, 1)
    onward(0, -1)
    for s in (1, -1):
        got_p(0, 2 * s, 1)
    prepare_p("next")
    tile(a_slots(0), p_slots("next"))

    for s in (1, -1):
        got_p(1, s, 0)
        to_sibling(1, s)
    got_a(2, 0)
    a_along_x(2)
    for dz in (-1, 1):
        for d in (1, -1, 2):
            got_a(dz, d)
        prepare_a(dz)
        tile(a_slots(dz), p_slots("near", "next"))
        if dz == -1:
            onward(1, 1)
            onward(1, -1)
            for d in (3, -3, 4):
                got_p(0, d, 0)
                to_sibling(0, d)
    for s in (1, -1):
        got_p(1, s, 1)
    prepare_p("pair_near")
    tile(a_slots(0, -1, 1), p_slots("pair_near"))

    for d in (1, -1, 2):
        got_a(2, d)
    prepare_a(2)
    tile(a_slots(2), p_slots("near", "next", "pair_near"))

    for d in (3, -3, 4):
        got_p(1, d, 0)
        to_sibling(1, d)
    for d in (3, -3, 4):
        got_p(0, d, 1)
    prepare_p("far")
    for d in (2, -2):
        got_p(1, d, 1)
    prepare_p("pair_next")
    for d in (3, -3, 4):
        got_p(1, d, 1)
    prepare_p("pair_far")
    got_p(0, 0, 1)
    got_p(1, 0, 1)
    prepare_p("home")
    tile(a_slots(2), p_slots("home"))
    tile(a_slots(2), p_slots("far", "pair_next", "pair_far"))

    @pl.when(c == r // 2)
    def _():
        diagonal()

    core_sums("near", "next", "pair_near")
    x_sums(2)
    others = a_slots(0, -1, 1)
    tile(others, p_slots("far"))
    core_sums("far")
    y_sums("near", "next", "pair_near")
    tile(others, p_slots("pair_far"))
    core_sums("pair_far")
    y_sums("far")
    zh_sum(2)
    tile(others, p_slots("pair_next"))
    core_sums("pair_next")
    y_sums("pair_far")
    tile(a_slots(-1), p_slots("home"))
    x_sums(-1)
    y_sums("pair_next")
    tile(a_slots(1), p_slots("home"))
    x_sums(1)
    tile(a_slots(0), p_slots("home"))
    core_sums("home")
    x_sums(0)
    zh_sum(-1)
    zh_sum(1)
    send_sum(("z",), y_total(1), z_pair)
    total_a = x_total(0)
    for dz in (2, 1, 3):
        total_a += arrived("zh", dz)
    da_out[...] = 5.0 * total_a
    total_p = y_total(0) + arrived("z")
    dp_out[...] = 5.0 * total_p.T
    for copy in copies.values():
        copy.wait_send()


def on_device(anchors, positives, row_lse, column_logsumexp):
    vmem = pl.BlockSpec(memory_space=pltpu.VMEM)
    anywhere = pl.BlockSpec(memory_space=pl.ANY)
    block = jax.ShapeDtypeStruct((BLOCK, WIDTH), f32)
    return pl.pallas_call(
        kernel,
        out_shape=(block, block),
        in_specs=[anywhere, anywhere, vmem, vmem],
        out_specs=(vmem, vmem),
        scratch_shapes=[
            pltpu.VMEM((ROWS, SENT, WIDTH), bf16),
            pltpu.VMEM((COLUMNS, SENT, WIDTH), bf16),
            pltpu.VMEM((WIDTH, ROWS * BLOCK), bf16),
            pltpu.VMEM((ROWS * BLOCK, BLOCK), f32),
            pltpu.VMEM((8, COLUMNS * BLOCK), f32),
            pltpu.VMEM((ROWS * BLOCK, WIDTH), f32),
            pltpu.VMEM((WIDTH, COLUMNS * BLOCK), f32),
            pltpu.VMEM((len(SUM_KEYS), BLOCK, WIDTH), bf16),
            pltpu.VMEM((len(SUM_KEYS), BLOCK, WIDTH), bf16),
            pltpu.SemaphoreType.DMA((len(SEM),)),
            pltpu.SemaphoreType.DMA((len(SEM),)),
            pltpu.SemaphoreType.DMA((2,)),
        ],
        compiler_params=pltpu.CompilerParams(
            collective_id=0, has_side_effects=True, vmem_limit_bytes=48 * 2**20
        ),
        name="infonce_backward",
    )(anchors, positives, row_lse.reshape(1, BLOCK), column_logsumexp.reshape(1, BLOCK))


def solution(mesh):
    return jax.shard_map(
        on_device,
        mesh=mesh,
        in_specs=(
            P(("row", "col"), None),
            P(("col", "row"), None),
            P(("row", "col")),
            P(("col", "row")),
        ),
        out_specs=(P(("row", "col"), None), P(("col", "row"), None)),
        check_vma=False,
    )
```

```python
import jax
import jax.numpy as jnp
from jax import lax
from jax.experimental import pallas as pl
from jax.experimental.pallas import tpu as pltpu
from jax.sharding import PartitionSpec as P

f32, bf16 = jnp.float32, jnp.bfloat16
MESH = pl.DeviceIdType.MESH
WIDTH = 128
BLOCK = 128
SENT = 144
LOG2E = 1.4426950408889634
SCALE = 10.0 * LOG2E
TOP = 12.0
NUM_Y, NUM_X, NUM_ZH = 8, 4, 4
COLUMNS, ROWS = 32, 16

P_GROUPS = {
    "home": [(0, 0), (1, 0)],
    "near": [(0, -1), (0, 1)],
    "next": [(0, -2), (0, 2)],
    "pair_near": [(1, -1), (1, 1)],
    "far": [(0, -3), (0, 3), (0, 4)],
    "pair_next": [(1, -2), (1, 2)],
    "pair_far": [(1, -3), (1, 3), (1, 4)],
}
P_KEYS = [(j, dy % NUM_Y, kk) for group in P_GROUPS.values() for j, dy in group for kk in (0, 1)]
A_KEYS = [(dz % NUM_ZH, dx % NUM_X) for dz in (0, -1, 1, 2) for dx in (0, -1, 1, 2)]
P_SLOT = {key: i for i, key in enumerate(P_KEYS)}
A_SLOT = {key: i for i, key in enumerate(A_KEYS)}


def ps(j, dy, kk):
    return P_SLOT[j, dy % NUM_Y, kk]


def as_(dz, dx):
    return A_SLOT[dz % NUM_ZH, dx % NUM_X]


def p_slots(*names):
    slots = [ps(j, dy, kk) for name in names for j, dy in P_GROUPS[name] for kk in (0, 1)]
    assert slots == list(range(slots[0], slots[0] + len(slots)))
    return slots[0], len(slots)


def a_slots(*dzs):
    slots = [as_(dz, dx) for dz in dzs for dx in (0, -1, 1, 2)]
    assert slots == list(range(slots[0], slots[0] + len(slots)))
    return slots[0], len(slots)


def numbering():
    keys = []
    keys += [("p", i) for i in range(1, COLUMNS)]
    keys += [("a", i) for i in range(1, ROWS)]
    keys += [("core", j, dy) for j in (0, 1) for dy in range(NUM_Y)]
    keys += [("z", dy % NUM_Y) for dy in (-2, -1, 0, 1, 2)]
    keys += [("pair", dy % NUM_Y) for dy in (3, 4, -3)]
    keys += [("y", dy) for dy in range(1, NUM_Y)]
    keys += [("x", dz, dx) for dz in range(NUM_ZH) for dx in range(1, NUM_X)]
    keys += [("zh", dz) for dz in range(1, NUM_ZH)]
    return {key: i for i, key in enumerate(keys)}


SEM = numbering()
SUM_KEYS = [k for k in SEM if k[0] not in ("p", "a")]
SUM_SLOT = {key: i for i, key in enumerate(SUM_KEYS)}

BARRIER_Y, BARRIER_ZH = (1, 2, 6, 7), (1, 3)


def kernel(
    a_ref, p_ref, la_ref, lp_ref, da_out, dp_out,
    ab, pb, at, ub, vb, acc_a, acc_p, out_s, in_s, send_sem, recv_sem, load_sem,
):
    loads = [
        pltpu.make_async_copy(a_ref, ab.at[0, pl.ds(0, BLOCK)], load_sem.at[0]),
        pltpu.make_async_copy(p_ref, pb.at[0, pl.ds(0, BLOCK)], load_sem.at[1]),
    ]
    for load in loads:
        load.start()

    r, c = lax.axis_index("row"), lax.axis_index("col")
    core, y, zl = r % 2, (r // 2) % NUM_Y, r // 16
    x, zh = c % NUM_X, c // NUM_X

    def row_dev(zl_, y_, core_):
        return (zl_ * 16 + y_ * 2 + core_, c)

    def col_dev(zh_, x_):
        return (r, zh_ * NUM_X + x_)

    sibling = row_dev(zl, y, 1 - core)
    z_pair = row_dev(1 - zl, y, core)
    y_dev = {d: row_dev(zl, (y + d) % NUM_Y, core) for d in range(1, NUM_Y)}
    pair_dev = {d: row_dev(1 - zl, (y + d) % NUM_Y, core) for d in range(1, NUM_Y)}
    x_dev = {d: col_dev(zh, (x + d) % NUM_X) for d in range(1, NUM_X)}
    zh_dev = {d: col_dev((zh + d) % NUM_ZH, x) for d in range(1, NUM_ZH)}

    peers = [sibling, z_pair, *x_dev.values()]
    peers += [y_dev[d] for d in BARRIER_Y] + [zh_dev[d] for d in BARRIER_ZH]
    barrier = pltpu.get_barrier_semaphore()
    for dev in peers:
        pl.semaphore_signal(barrier, inc=1, device_id=dev, device_id_type=MESH)
    ab[0, BLOCK:, :] = jnp.broadcast_to(la_ref[...], (SENT - BLOCK, WIDTH))
    pb[0, BLOCK:, :] = jnp.broadcast_to(lp_ref[...], (SENT - BLOCK, WIDTH))
    for load in loads:
        load.wait()
    pl.semaphore_wait(barrier, len(peers))

    copies = {}

    def send(key, src, dst, dev):
        copy = pltpu.make_async_remote_copy(
            src_ref=src, dst_ref=dst, send_sem=send_sem.at[SEM[key]], recv_sem=recv_sem.at[SEM[key]],
            device_id=dev, device_id_type=MESH,
        )
        copy.start()
        copies[key] = copy

    def got(key):
        copies[key].wait_recv()

    def send_p(src, dst, dev):
        send(("p", dst), pb.at[src], pb.at[dst], dev)

    def send_a(src, dst, dev):
        send(("a", dst), ab.at[src], ab.at[dst], dev)

    def got_p(j, dy, kk):
        got(("p", ps(j, dy, kk)))

    def got_a(dz, dx):
        got(("a", as_(dz, dx)))

    def a_along_x(dz):
        for d in (1, -1, 2):
            send_a(as_(dz, 0), as_(dz, -d), x_dev[d % NUM_X])

    def p_along_y(ds):
        for d in ds:
            send_p(ps(0, 0, 0), ps(0, -d, 0), y_dev[d % NUM_Y])

    def to_sibling(j, dy):
        send_p(ps(j, dy, 0), ps(j, dy, 1), sibling)

    def to_pair(dy):
        send_p(ps(0, dy, 0), ps(1, dy, 0), z_pair)

    def spread(dy):
        got_p(0, dy, 0)
        to_pair(dy)
        to_sibling(0, dy)

    def from_pair(dy):
        got_p(1, dy, 0)
        to_sibling(1, dy)

    def onward():
        for s in (1, -1):
            got_p(0, -2 * s, 0)
            send_p(ps(0, -2 * s, 0), ps(0, -3 * s, 0), y_dev[s % NUM_Y])
        source = jnp.where(core == 0, ps(0, -2, 0), ps(0, 2, 0))
        send_p(source, ps(0, 4, 0), row_dev(zl, (y + jnp.where(core == 0, 2, 6)) % NUM_Y, core))
        for s in (1, -1):
            to_pair(-2 * s)
            to_sibling(0, -2 * s)

    def prepare_a(dz):
        first, count = a_slots(dz)
        for i in range(first, first + count):
            rows = slice(i * BLOCK, (i + 1) * BLOCK)
            at[:, rows] = ab[i, :BLOCK, :].astype(f32).T.astype(bf16)
            lse = ab[i, BLOCK:, :].astype(f32)[0:1, :]
            ub[rows, :] = jnp.broadcast_to(jnp.exp(TOP - lse), (BLOCK, BLOCK)).T

    def prepare_p(name):
        first, count = p_slots(name)
        for i in range(first, first + count):
            lse = pb[i, BLOCK:, :].astype(f32)[0:8, :]
            vb[:, i * BLOCK:(i + 1) * BLOCK] = jnp.exp(TOP - lse)

    touched = set()

    def tile(row_slots, col_slots):
        (r0, nr), (c0, nc) = row_slots, col_slots
        rows, cols = slice(r0 * BLOCK, (r0 + nr) * BLOCK), slice(c0 * BLOCK, (c0 + nc) * BLOCK)
        a = ab[r0:r0 + nr, :BLOCK, :].reshape(nr * BLOCK, WIDTH)
        p = pb[c0:c0 + nc, :BLOCK, :].reshape(nc * BLOCK, WIDTH)
        t = lax.dot_general(a, p, (((1,), (1,)), ((), ())), preferred_element_type=f32)
        weight = jnp.concatenate([ub[rows, :]] * nc, axis=1) + vb[0:1, cols]
        soft = (jnp.exp2(t * SCALE - TOP * LOG2E) * weight).astype(bf16)
        to_rows = jnp.dot(soft, p, preferred_element_type=f32)
        to_cols = jnp.dot(at[:, rows], soft, preferred_element_type=f32)
        row_keys = {("a", i) for i in range(r0, r0 + nr)}
        col_keys = {("p", i) for i in range(c0, c0 + nc)}
        if row_keys <= touched:
            acc_a[rows, :] += to_rows
        else:
            assert not row_keys & touched
            acc_a[rows, :] = to_rows
        if col_keys <= touched:
            acc_p[:, cols] += to_cols
        else:
            assert not col_keys & touched
            acc_p[:, cols] = to_cols
        touched.update(row_keys | col_keys)

    def own_a(dz, dx):
        i = as_(dz, dx)
        return acc_a[i * BLOCK:(i + 1) * BLOCK, :]

    def own_p(j, dy, kk):
        i = ps(j, dy, kk)
        return acc_p[:, i * BLOCK:(i + 1) * BLOCK]

    def send_sum(key, value, dev):
        i = SUM_SLOT[key]
        out_s[i] = value.astype(bf16)
        send(key, out_s.at[i], in_s.at[i], dev)

    def arrived(*key):
        got(key)
        return in_s[SUM_SLOT[key]].astype(f32)

    def core_sums(*names):
        for name in names:
            for j, dy in P_GROUPS[name]:
                send_sum(("core", j, dy % NUM_Y), own_p(j, dy, 1), sibling)

    def chip_sum(j, dy):
        return own_p(j, dy, 0) + arrived("core", j, dy % NUM_Y)

    def z_sums(*names):
        for name in names:
            for j, dy in P_GROUPS[name]:
                if j == 1:
                    send_sum(("z", dy % NUM_Y), chip_sum(1, dy), z_pair)

    def pair_far_sums():
        for j, dy in P_GROUPS["pair_far"]:
            send_sum(("pair", dy % NUM_Y), chip_sum(j, dy), pair_dev[dy % NUM_Y])

    def pair_sum(dy):
        if dy in (3, -3, 4):
            return chip_sum(0, dy)
        return chip_sum(0, dy) + arrived("z", dy % NUM_Y)

    def y_sums(name):
        for _, dy in P_GROUPS[name]:
            send_sum(("y", dy % NUM_Y), pair_sum(dy), y_dev[dy % NUM_Y])

    def x_sums(dz):
        for dx in (2, 1, -1):
            send_sum(("x", dz % NUM_ZH, dx % NUM_X), own_a(dz, dx), x_dev[dx % NUM_X])

    def x_total(dz):
        total = own_a(dz, 0)
        for dx in range(1, NUM_X):
            total += arrived("x", dz % NUM_ZH, dx)
        return total

    def zh_sum(dz):
        send_sum(("zh", dz % NUM_ZH), x_total(dz), zh_dev[dz % NUM_ZH])

    def diagonal(*names):
        for name in names:
            for j, dy in P_GROUPS[name]:

                @pl.when((c == r // 2) & ((core + zl) % 2 == j))
                def _():
                    for kk in (0, 1):
                        k = ps(j, dy, kk)
                        other = (y + dy + NUM_Y) % NUM_Y * 2 + (core + kk) % 2
                        dz, dx = (other // NUM_X + NUM_ZH - zh) % NUM_ZH, (other % NUM_X + NUM_X - x) % NUM_X
                        i = NUM_X * jnp.where(dz <= 1, 2 * dz, 7 - 2 * dz) + jnp.where(dx <= 1, 2 * dx, 7 - 2 * dx)
                        rows = pl.ds(pl.multiple_of(i * BLOCK, BLOCK), BLOCK)
                        cols = slice(k * BLOCK, (k + 1) * BLOCK)
                        acc_a[rows, :] -= 2.0 * pb[k, :BLOCK, :].astype(f32)
                        acc_p[:, cols] -= 2.0 * at[:, rows].astype(f32)

    def sums_of(*names):
        diagonal(*names)
        core_sums(*names)

    send_a(as_(0, 0), as_(-1, 0), zh_dev[1])
    send_a(as_(0, 0), as_(1, 0), zh_dev[3])
    p_along_y((2, -2, 1, -1))
    to_pair(0)
    a_along_x(0)
    to_sibling(0, 0)

    for s in (1, -1):
        spread(s)
    from_pair(0)
    got_a(-1, 0)
    send_a(as_(-1, 0), as_(2, 0), zh_dev[1])
    a_along_x(-1)
    got_a(1, 0)
    a_along_x(1)
    onward()
    for d in (1, -1, 2):
        got_a(0, d)
    prepare_a(0)
    for s in (1, -1):
        got_p(0, s, 1)
    prepare_p("near")
    tile(a_slots(0), p_slots("near"))
    for s in (1, -1):
        got_p(0, 2 * s, 1)
    prepare_p("next")
    tile(a_slots(0), p_slots("next"))
    for s in (1, -1):
        from_pair(s)
    got_a(2, 0)
    a_along_x(2)
    for d in (1, -1, 2):
        got_a(-1, d)
    prepare_a(-1)
    tile(a_slots(-1), p_slots("near", "next"))
    for s in (1, -1):
        from_pair(2 * s)
    for d in (3, -3, 4):
        spread(d)
    for d in (1, -1, 2):
        got_a(1, d)
    prepare_a(1)
    tile(a_slots(1), p_slots("near", "next"))
    for s in (1, -1):
        got_p(1, s, 1)
    prepare_p("pair_near")
    tile(a_slots(0, -1, 1), p_slots("pair_near"))
    for d in (3, -3, 4):
        from_pair(d)
    for d in (1, -1, 2):
        got_a(2, d)
    prepare_a(2)
    tile(a_slots(2), p_slots("near", "next", "pair_near"))
    sums_of("pair_near", "next", "near")

    for s in (1, -1):
        got_p(1, 2 * s, 1)
    prepare_p("pair_next")
    tile(a_slots(0, -1, 1, 2), p_slots("pair_next"))
    sums_of("pair_next")
    z_sums("pair_near")
    for d in (3, -3, 4):
        got_p(1, d, 1)
    prepare_p("pair_far")
    tile(a_slots(0, -1, 1, 2), p_slots("pair_far"))
    sums_of("pair_far")
    z_sums("pair_next")
    for d in (3, -3, 4):
        got_p(0, d, 1)
    prepare_p("far")
    got_p(0, 0, 1)
    got_p(1, 0, 1)
    prepare_p("home")
    tile(a_slots(2), p_slots("far"))
    tile(a_slots(2), p_slots("home"))
    diagonal("far", "home")
    x_sums(2)
    y_sums("near")
    pair_far_sums()
    tile(a_slots(-1), p_slots("far"))
    tile(a_slots(-1), p_slots("home"))
    x_sums(-1)
    y_sums("next")
    tile(a_slots(1), p_slots("far"))
    tile(a_slots(1), p_slots("home"))
    x_sums(1)
    tile(a_slots(0), p_slots("far"))
    core_sums("far")
    zh_sum(2)
    tile(a_slots(0), p_slots("home"))
    core_sums("home")
    x_sums(0)
    y_sums("far")
    zh_sum(-1)
    z_sums("home")
    zh_sum(1)
    total_p = pair_sum(0)
    for dy in (1, -1, 2, -2, 3, -3, 4):
        total_p += arrived("y", dy % NUM_Y)
    for dy in (3, -3, 4):
        total_p += arrived("pair", dy % NUM_Y)
    dp_out[...] = 5.0 * total_p.T
    total_a = x_total(0)
    for dz in (2, 3, 1):
        total_a += arrived("zh", dz)
    da_out[...] = 5.0 * total_a
    for copy in copies.values():
        copy.wait_send()


def on_device(anchors, positives, row_lse, column_logsumexp):
    vmem = pl.BlockSpec(memory_space=pltpu.VMEM)
    anywhere = pl.BlockSpec(memory_space=pltpu.HBM)
    block = jax.ShapeDtypeStruct((BLOCK, WIDTH), f32)
    return pl.pallas_call(
        kernel,
        out_shape=(block, block),
        in_specs=[anywhere, anywhere, vmem, vmem],
        out_specs=(vmem, vmem),
        scratch_shapes=[
            pltpu.VMEM((ROWS, SENT, WIDTH), bf16),
            pltpu.VMEM((COLUMNS, SENT, WIDTH), bf16),
            pltpu.VMEM((WIDTH, ROWS * BLOCK), bf16),
            pltpu.VMEM((ROWS * BLOCK, BLOCK), f32),
            pltpu.VMEM((8, COLUMNS * BLOCK), f32),
            pltpu.VMEM((ROWS * BLOCK, WIDTH), f32),
            pltpu.VMEM((WIDTH, COLUMNS * BLOCK), f32),
            pltpu.VMEM((len(SUM_KEYS), BLOCK, WIDTH), bf16),
            pltpu.VMEM((len(SUM_KEYS), BLOCK, WIDTH), bf16),
            pltpu.SemaphoreType.DMA((len(SEM),)),
            pltpu.SemaphoreType.DMA((len(SEM),)),
            pltpu.SemaphoreType.DMA((2,)),
        ],
        compiler_params=pltpu.CompilerParams(
            collective_id=0, has_side_effects=True, vmem_limit_bytes=63 * 2**20
        ),
        name="infonce_backward",
    )(anchors, positives, row_lse.reshape(1, BLOCK), column_logsumexp.reshape(1, BLOCK))


def solution(mesh):
    return jax.shard_map(
        on_device,
        mesh=mesh,
        in_specs=(
            P(("row", "col"), None),
            P(("col", "row"), None),
            P(("row", "col")),
            P(("col", "row")),
        ),
        out_specs=(P(("row", "col"), None), P(("col", "row"), None)),
        check_vma=False,
    )
```

```python
import jax
import jax.numpy as jnp
from jax import lax
from jax.experimental import pallas as pl
from jax.experimental.pallas import tpu as pltpu
from jax.sharding import PartitionSpec as P

f32, bf16 = jnp.float32, jnp.bfloat16
MESH = pl.DeviceIdType.MESH
WIDTH = 128
BLOCK = 128
SENT = 144
LOG2E = 1.4426950408889634
SCALE = 10.0 * LOG2E
TOP = 12.0
NUM_Y, NUM_X, NUM_ZH = 8, 4, 4
COLUMNS, ROWS = 32, 16

P_GROUPS = {
    "home": [(0, 0), (1, 0)],
    "near": [(0, -1), (0, 1)],
    "next": [(0, -2), (0, 2)],
    "pair_near": [(1, -1), (1, 1)],
    "far": [(0, -3), (0, 3), (0, 4)],
    "pair_next": [(1, -2), (1, 2)],
    "pair_far": [(1, -3), (1, 3), (1, 4)],
}
P_KEYS = [(j, dy % NUM_Y, kk) for group in P_GROUPS.values() for j, dy in group for kk in (0, 1)]
A_KEYS = [(dz % NUM_ZH, dx % NUM_X) for dz in (0, -1, 1, 2) for dx in (0, -1, 1, 2)]
P_SLOT = {key: i for i, key in enumerate(P_KEYS)}
A_SLOT = {key: i for i, key in enumerate(A_KEYS)}


def ps(j, dy, kk):
    return P_SLOT[j, dy % NUM_Y, kk]


def as_(dz, dx):
    return A_SLOT[dz % NUM_ZH, dx % NUM_X]


def p_slots(*names):
    slots = [ps(j, dy, kk) for name in names for j, dy in P_GROUPS[name] for kk in (0, 1)]
    assert slots == list(range(slots[0], slots[0] + len(slots)))
    return slots[0], len(slots)


def a_slots(*dzs):
    slots = [as_(dz, dx) for dz in dzs for dx in (0, -1, 1, 2)]
    assert slots == list(range(slots[0], slots[0] + len(slots)))
    return slots[0], len(slots)


def numbering():
    keys = []
    keys += [("p", i) for i in range(1, COLUMNS)]
    keys += [("a", i) for i in range(1, ROWS)]
    keys += [("core", j, dy) for j in (0, 1) for dy in range(NUM_Y)]
    keys += [("z", dy % NUM_Y) for dy in (-2, -1, 0, 1, 2)]
    keys += [("pair", dy % NUM_Y) for dy in (3, 4, -3)]
    keys += [("y", dy) for dy in range(1, NUM_Y)]
    keys += [("x", dz, dx) for dz in range(NUM_ZH) for dx in range(1, NUM_X)]
    keys += [("zh", dz) for dz in range(1, NUM_ZH)]
    return {key: i for i, key in enumerate(keys)}


SEM = numbering()
SUM_KEYS = [k for k in SEM if k[0] not in ("p", "a")]
SUM_SLOT = {key: i for i, key in enumerate(SUM_KEYS)}

BARRIER_Y, BARRIER_ZH = (1, 2, 6, 7), (1, 3)


def kernel(
    a_ref, p_ref, la_ref, lp_ref, da_out, dp_out,
    ab, pb, at, ub, vb, acc_a, acc_p, out_s, in_s, la, lp, send_sem, recv_sem, load_sem,
):
    loads = [
        pltpu.make_async_copy(a_ref, ab.at[0, pl.ds(0, BLOCK)], load_sem.at[0]),
        pltpu.make_async_copy(p_ref, pb.at[0, pl.ds(0, BLOCK)], load_sem.at[1]),
        pltpu.make_async_copy(la_ref, la, load_sem.at[2]),
        pltpu.make_async_copy(lp_ref, lp, load_sem.at[3]),
    ]
    for load in loads:
        load.start()

    r, c = lax.axis_index("row"), lax.axis_index("col")
    core, y, zl = r % 2, (r // 2) % NUM_Y, r // 16
    x, zh = c % NUM_X, c // NUM_X

    def row_dev(zl_, y_, core_):
        return (zl_ * 16 + y_ * 2 + core_, c)

    def col_dev(zh_, x_):
        return (r, zh_ * NUM_X + x_)

    sibling = row_dev(zl, y, 1 - core)
    z_pair = row_dev(1 - zl, y, core)
    y_dev = {d: row_dev(zl, (y + d) % NUM_Y, core) for d in range(1, NUM_Y)}
    pair_dev = {d: row_dev(1 - zl, (y + d) % NUM_Y, core) for d in range(1, NUM_Y)}
    x_dev = {d: col_dev(zh, (x + d) % NUM_X) for d in range(1, NUM_X)}
    zh_dev = {d: col_dev((zh + d) % NUM_ZH, x) for d in range(1, NUM_ZH)}

    peers = [sibling, z_pair, *x_dev.values()]
    peers += [y_dev[d] for d in BARRIER_Y] + [zh_dev[d] for d in BARRIER_ZH]
    barrier = pltpu.get_barrier_semaphore()
    for dev in peers:
        pl.semaphore_signal(barrier, inc=1, device_id=dev, device_id_type=MESH)
    for load in loads:
        load.wait()
    ab[0, BLOCK:, :] = jnp.broadcast_to(la[...], (SENT - BLOCK, WIDTH))
    pb[0, BLOCK:, :] = jnp.broadcast_to(lp[...], (SENT - BLOCK, WIDTH))
    pl.semaphore_wait(barrier, len(peers))

    copies = {}

    def send(key, src, dst, dev):
        copy = pltpu.make_async_remote_copy(
            src_ref=src, dst_ref=dst, send_sem=send_sem.at[SEM[key]], recv_sem=recv_sem.at[SEM[key]],
            device_id=dev, device_id_type=MESH,
        )
        copy.start()
        copies[key] = copy

    def got(key):
        copies[key].wait_recv()

    def send_p(src, dst, dev):
        send(("p", dst), pb.at[src], pb.at[dst], dev)

    def send_a(src, dst, dev):
        send(("a", dst), ab.at[src], ab.at[dst], dev)

    def got_p(j, dy, kk):
        got(("p", ps(j, dy, kk)))

    def got_a(dz, dx):
        got(("a", as_(dz, dx)))

    def a_along_x(dz):
        for d in (1, -1, 2):
            send_a(as_(dz, 0), as_(dz, -d), x_dev[d % NUM_X])

    def p_along_y(ds):
        for d in ds:
            send_p(ps(0, 0, 0), ps(0, -d, 0), y_dev[d % NUM_Y])

    def to_sibling(j, dy):
        send_p(ps(j, dy, 0), ps(j, dy, 1), sibling)

    def to_pair(dy):
        send_p(ps(0, dy, 0), ps(1, dy, 0), z_pair)

    def spread(dy):
        got_p(0, dy, 0)
        to_pair(dy)
        to_sibling(0, dy)

    def from_pair(dy):
        got_p(1, dy, 0)
        to_sibling(1, dy)

    def onward():
        for s in (1, -1):
            got_p(0, -2 * s, 0)
            send_p(ps(0, -2 * s, 0), ps(0, -3 * s, 0), y_dev[s % NUM_Y])
        source = jnp.where(core == 0, ps(0, -2, 0), ps(0, 2, 0))
        send_p(source, ps(0, 4, 0), row_dev(zl, (y + jnp.where(core == 0, 2, 6)) % NUM_Y, core))
        for s in (1, -1):
            to_pair(-2 * s)
            to_sibling(0, -2 * s)

    def prepare_a(dz):
        first, count = a_slots(dz)
        for i in range(first, first + count):
            rows = slice(i * BLOCK, (i + 1) * BLOCK)
            at[:, rows] = ab[i, :BLOCK, :].T
            lse = ab[i, BLOCK:, :].astype(f32)[0:1, :]
            ub[rows, :] = jnp.broadcast_to(jnp.exp(TOP - lse), (BLOCK, BLOCK)).T

    def prepare_p(name):
        first, count = p_slots(name)
        for i in range(first, first + count):
            lse = pb[i, BLOCK:, :].astype(f32)[0:8, :]
            vb[:, i * BLOCK:(i + 1) * BLOCK] = jnp.exp(TOP - lse)

    touched = set()

    def tile(row_slots, col_slots):
        (r0, nr), (c0, nc) = row_slots, col_slots
        rows, cols = slice(r0 * BLOCK, (r0 + nr) * BLOCK), slice(c0 * BLOCK, (c0 + nc) * BLOCK)
        a = ab[r0:r0 + nr, :BLOCK, :].reshape(nr * BLOCK, WIDTH)
        p = pb[c0:c0 + nc, :BLOCK, :].reshape(nc * BLOCK, WIDTH)
        t = lax.dot_general(a, p, (((1,), (1,)), ((), ())), preferred_element_type=f32)
        weight = jnp.concatenate([ub[rows, :]] * nc, axis=1) + vb[0:1, cols]
        soft = (jnp.exp2(t * SCALE - TOP * LOG2E) * weight).astype(bf16)
        to_rows = jnp.dot(soft, p, preferred_element_type=f32)
        to_cols = jnp.dot(at[:, rows], soft, preferred_element_type=f32)
        row_keys = {("a", i) for i in range(r0, r0 + nr)}
        col_keys = {("p", i) for i in range(c0, c0 + nc)}
        if row_keys <= touched:
            acc_a[rows, :] += to_rows
        else:
            assert not row_keys & touched
            acc_a[rows, :] = to_rows
        if col_keys <= touched:
            acc_p[:, cols] += to_cols
        else:
            assert not col_keys & touched
            acc_p[:, cols] = to_cols
        touched.update(row_keys | col_keys)

    def own_a(dz, dx):
        i = as_(dz, dx)
        return acc_a[i * BLOCK:(i + 1) * BLOCK, :]

    def own_p(j, dy, kk):
        i = ps(j, dy, kk)
        return acc_p[:, i * BLOCK:(i + 1) * BLOCK]

    def send_sum(key, value, dev):
        i = SUM_SLOT[key]
        out_s[i] = value.astype(bf16)
        send(key, out_s.at[i], in_s.at[i], dev)

    def arrived(*key):
        got(key)
        return in_s[SUM_SLOT[key]].astype(f32)

    def core_sums(*names):
        for name in names:
            for j, dy in P_GROUPS[name]:
                send_sum(("core", j, dy % NUM_Y), own_p(j, dy, 1), sibling)

    def chip_sum(j, dy):
        return own_p(j, dy, 0) + arrived("core", j, dy % NUM_Y)

    def z_sums(*names):
        for name in names:
            for j, dy in P_GROUPS[name]:
                if j == 1:
                    send_sum(("z", dy % NUM_Y), chip_sum(1, dy), z_pair)

    def pair_far_sums():
        for j, dy in P_GROUPS["pair_far"]:
            send_sum(("pair", dy % NUM_Y), chip_sum(j, dy), pair_dev[dy % NUM_Y])

    def pair_sum(dy):
        if dy in (3, -3, 4):
            return chip_sum(0, dy)
        return chip_sum(0, dy) + arrived("z", dy % NUM_Y)

    def y_sums(name):
        for _, dy in P_GROUPS[name]:
            send_sum(("y", dy % NUM_Y), pair_sum(dy), y_dev[dy % NUM_Y])

    def x_sums(dz):
        for dx in (2, 1, -1):
            send_sum(("x", dz % NUM_ZH, dx % NUM_X), own_a(dz, dx), x_dev[dx % NUM_X])

    def x_total(dz):
        total = own_a(dz, 0)
        for dx in range(1, NUM_X):
            total += arrived("x", dz % NUM_ZH, dx)
        return total

    def zh_sum(dz):
        send_sum(("zh", dz % NUM_ZH), x_total(dz), zh_dev[dz % NUM_ZH])

    def diagonal(*names):
        for name in names:
            for j, dy in P_GROUPS[name]:

                @pl.when((c == r // 2) & ((core + zl) % 2 == j))
                def _():
                    for kk in (0, 1):
                        k = ps(j, dy, kk)
                        other = (y + dy + NUM_Y) % NUM_Y * 2 + (core + kk) % 2
                        dz, dx = (other // NUM_X + NUM_ZH - zh) % NUM_ZH, (other % NUM_X + NUM_X - x) % NUM_X
                        i = NUM_X * jnp.where(dz <= 1, 2 * dz, 7 - 2 * dz) + jnp.where(dx <= 1, 2 * dx, 7 - 2 * dx)
                        rows = pl.ds(pl.multiple_of(i * BLOCK, BLOCK), BLOCK)
                        cols = slice(k * BLOCK, (k + 1) * BLOCK)
                        acc_a[rows, :] -= 2.0 * pb[k, :BLOCK, :].astype(f32)
                        acc_p[:, cols] -= 2.0 * at[:, rows].astype(f32)

    def sums_of(*names):
        diagonal(*names)
        core_sums(*names)

    send_a(as_(0, 0), as_(-1, 0), zh_dev[1])
    send_a(as_(0, 0), as_(1, 0), zh_dev[3])
    p_along_y((2, -2, 1, -1))
    to_pair(0)
    a_along_x(0)
    to_sibling(0, 0)

    for s in (1, -1):
        spread(s)
    from_pair(0)
    got_a(-1, 0)
    send_a(as_(-1, 0), as_(2, 0), zh_dev[1])
    a_along_x(-1)
    got_a(1, 0)
    a_along_x(1)
    onward()
    for d in (1, -1, 2):
        got_a(0, d)
    prepare_a(0)
    for s in (1, -1):
        got_p(0, s, 1)
    prepare_p("near")
    tile(a_slots(0), p_slots("near"))
    for s in (1, -1):
        got_p(0, 2 * s, 1)
    prepare_p("next")
    tile(a_slots(0), p_slots("next"))
    for s in (1, -1):
        from_pair(s)
    got_a(2, 0)
    a_along_x(2)
    for d in (1, -1, 2):
        got_a(-1, d)
    prepare_a(-1)
    tile(a_slots(-1), p_slots("near", "next"))
    for s in (1, -1):
        from_pair(2 * s)
    for d in (3, -3, 4):
        spread(d)
    for d in (1, -1, 2):
        got_a(1, d)
    prepare_a(1)
    tile(a_slots(1), p_slots("near", "next"))
    for s in (1, -1):
        got_p(1, s, 1)
    prepare_p("pair_near")
    tile(a_slots(0, -1, 1), p_slots("pair_near"))
    for d in (3, -3, 4):
        from_pair(d)
    for d in (1, -1, 2):
        got_a(2, d)
    prepare_a(2)
    tile(a_slots(2), p_slots("near", "next", "pair_near"))
    sums_of("pair_near", "next", "near")

    for s in (1, -1):
        got_p(1, 2 * s, 1)
    prepare_p("pair_next")
    tile(a_slots(0, -1, 1, 2), p_slots("pair_next"))
    sums_of("pair_next")
    z_sums("pair_near")
    for d in (3, -3, 4):
        got_p(1, d, 1)
    prepare_p("pair_far")
    tile(a_slots(0, -1, 1, 2), p_slots("pair_far"))
    sums_of("pair_far")
    z_sums("pair_next")
    for d in (3, -3, 4):
        got_p(0, d, 1)
    prepare_p("far")
    got_p(0, 0, 1)
    got_p(1, 0, 1)
    prepare_p("home")
    tile(a_slots(2), p_slots("far"))
    tile(a_slots(2), p_slots("home"))
    diagonal("far", "home")
    x_sums(2)
    y_sums("near")
    pair_far_sums()
    tile(a_slots(-1), p_slots("far"))
    tile(a_slots(-1), p_slots("home"))
    x_sums(-1)
    tile(a_slots(1), p_slots("far"))
    tile(a_slots(1), p_slots("home"))
    x_sums(1)
    y_sums("next")
    tile(a_slots(0), p_slots("far"))
    core_sums("far")
    tile(a_slots(0), p_slots("home"))
    core_sums("home")
    x_sums(0)
    y_sums("far")
    z_sums("home")
    zh_sum(2)
    zh_sum(-1)
    zh_sum(1)
    total_p = pair_sum(0)
    for dy in (1, -1, 2, -2, 3, -3, 4):
        total_p += arrived("y", dy % NUM_Y)
    for dy in (3, -3, 4):
        total_p += arrived("pair", dy % NUM_Y)
    dp_out[...] = 5.0 * total_p.T
    total_a = x_total(0)
    for dz in (2, 3, 1):
        total_a += arrived("zh", dz)
    da_out[...] = 5.0 * total_a
    for copy in copies.values():
        copy.wait_send()


def on_device(anchors, positives, row_lse, column_logsumexp):
    vmem = pl.BlockSpec(memory_space=pltpu.VMEM)
    anywhere = pl.BlockSpec(memory_space=pltpu.HBM)
    block = jax.ShapeDtypeStruct((BLOCK, WIDTH), f32)
    return pl.pallas_call(
        kernel,
        out_shape=(block, block),
        in_specs=[anywhere] * 4,
        out_specs=(vmem, vmem),
        scratch_shapes=[
            pltpu.VMEM((ROWS, SENT, WIDTH), bf16),
            pltpu.VMEM((COLUMNS, SENT, WIDTH), bf16),
            pltpu.VMEM((WIDTH, ROWS * BLOCK), bf16),
            pltpu.VMEM((ROWS * BLOCK, BLOCK), f32),
            pltpu.VMEM((8, COLUMNS * BLOCK), f32),
            pltpu.VMEM((ROWS * BLOCK, WIDTH), f32),
            pltpu.VMEM((WIDTH, COLUMNS * BLOCK), f32),
            pltpu.VMEM((len(SUM_KEYS), BLOCK, WIDTH), bf16),
            pltpu.VMEM((len(SUM_KEYS), BLOCK, WIDTH), bf16),
            pltpu.VMEM((1, BLOCK), bf16),
            pltpu.VMEM((1, BLOCK), bf16),
            pltpu.SemaphoreType.DMA((len(SEM),)),
            pltpu.SemaphoreType.DMA((len(SEM),)),
            pltpu.SemaphoreType.DMA((4,)),
        ],
        compiler_params=pltpu.CompilerParams(
            collective_id=0, has_side_effects=True, vmem_limit_bytes=63 * 2**20
        ),
        name="infonce_backward",
    )(anchors, positives, row_lse.reshape(1, BLOCK), column_logsumexp.reshape(1, BLOCK))


def solution(mesh):
    return jax.shard_map(
        on_device,
        mesh=mesh,
        in_specs=(
            P(("row", "col"), None),
            P(("col", "row"), None),
            P(("row", "col")),
            P(("col", "row")),
        ),
        out_specs=(P(("row", "col"), None), P(("col", "row"), None)),
        check_vma=False,
    )
```

```python
import jax
import jax.numpy as jnp
from jax import lax
from jax.experimental import pallas as pl
from jax.experimental.pallas import tpu as pltpu
from jax.sharding import PartitionSpec as P

f32, bf16 = jnp.float32, jnp.bfloat16
MESH = pl.DeviceIdType.MESH
WIDTH = 128
BLOCK = 128
SENT = 144
LOG2E = 1.4426950408889634
SCALE = 10.0 * LOG2E
TOP = 12.0
NUM_Y, NUM_X, NUM_ZH = 8, 4, 4
COLUMNS, ROWS = 32, 16

P_GROUPS = {
    "home": [(0, 0), (1, 0)],
    "near": [(0, -1), (0, 1)],
    "next": [(0, -2), (0, 2)],
    "pair_near": [(1, -1), (1, 1)],
    "far": [(0, -3), (0, 3), (0, 4)],
    "pair_next": [(1, -2), (1, 2)],
    "pair_far": [(1, -3), (1, 3), (1, 4)],
}
P_KEYS = [(j, dy % NUM_Y, kk) for group in P_GROUPS.values() for j, dy in group for kk in (0, 1)]
A_KEYS = [(dz % NUM_ZH, dx % NUM_X) for dz in (0, -1, 1, 2) for dx in (0, -1, 1, 2)]
P_SLOT = {key: i for i, key in enumerate(P_KEYS)}
A_SLOT = {key: i for i, key in enumerate(A_KEYS)}


def ps(j, dy, kk):
    return P_SLOT[j, dy % NUM_Y, kk]


def as_(dz, dx):
    return A_SLOT[dz % NUM_ZH, dx % NUM_X]


def p_slots(*names):
    slots = [ps(j, dy, kk) for name in names for j, dy in P_GROUPS[name] for kk in (0, 1)]
    assert slots == list(range(slots[0], slots[0] + len(slots)))
    return slots[0], len(slots)


def a_slots(*dzs):
    slots = [as_(dz, dx) for dz in dzs for dx in (0, -1, 1, 2)]
    assert slots == list(range(slots[0], slots[0] + len(slots)))
    return slots[0], len(slots)


def numbering():
    keys = []
    keys += [("p", i) for i in range(1, COLUMNS)]
    keys += [("a", i) for i in range(1, ROWS)]
    keys += [("core", j, dy) for j in (0, 1) for dy in range(NUM_Y)]
    keys += [("z", dy % NUM_Y) for dy in (-2, -1, 0, 1, 2)]
    keys += [("pair", dy % NUM_Y) for dy in (3, 4, -3)]
    keys += [("y", dy) for dy in range(1, NUM_Y)]
    keys += [("x", dz, dx) for dz in range(NUM_ZH) for dx in range(1, NUM_X)]
    keys += [("zh", dz) for dz in range(1, NUM_ZH)]
    return {key: i for i, key in enumerate(keys)}


SEM = numbering()
SUM_KEYS = [k for k in SEM if k[0] not in ("p", "a")]
SUM_SLOT = {key: i for i, key in enumerate(SUM_KEYS)}

BARRIER_Y, BARRIER_ZH = (1, 2, 6, 7), (1, 3)


def kernel(
    a_ref, p_ref, la_ref, lp_ref, da_out, dp_out,
    ab, pb, at, ub, vb, acc_a, acc_p, out_s, in_s, la, lp, send_sem, recv_sem, load_sem,
):
    loads = [
        pltpu.make_async_copy(a_ref, ab.at[0, pl.ds(0, BLOCK)], load_sem.at[0]),
        pltpu.make_async_copy(p_ref, pb.at[0, pl.ds(0, BLOCK)], load_sem.at[1]),
        pltpu.make_async_copy(la_ref, la, load_sem.at[2]),
        pltpu.make_async_copy(lp_ref, lp, load_sem.at[3]),
    ]
    for load in loads:
        load.start()

    r, c = lax.axis_index("row"), lax.axis_index("col")
    core, y, zl = r % 2, (r // 2) % NUM_Y, r // 16
    x, zh = c % NUM_X, c // NUM_X

    def row_dev(zl_, y_, core_):
        return (zl_ * 16 + y_ * 2 + core_, c)

    def col_dev(zh_, x_):
        return (r, zh_ * NUM_X + x_)

    sibling = row_dev(zl, y, 1 - core)
    z_pair = row_dev(1 - zl, y, core)
    y_dev = {d: row_dev(zl, (y + d) % NUM_Y, core) for d in range(1, NUM_Y)}
    pair_dev = {d: row_dev(1 - zl, (y + d) % NUM_Y, core) for d in range(1, NUM_Y)}
    x_dev = {d: col_dev(zh, (x + d) % NUM_X) for d in range(1, NUM_X)}
    zh_dev = {d: col_dev((zh + d) % NUM_ZH, x) for d in range(1, NUM_ZH)}

    peers = [sibling, z_pair, *x_dev.values()]
    peers += [y_dev[d] for d in BARRIER_Y] + [zh_dev[d] for d in BARRIER_ZH]
    barrier = pltpu.get_barrier_semaphore()
    for dev in peers:
        pl.semaphore_signal(barrier, inc=1, device_id=dev, device_id_type=MESH)
    for load in loads:
        load.wait()
    ab[0, BLOCK:, :] = jnp.broadcast_to(la[...], (SENT - BLOCK, WIDTH))
    pb[0, BLOCK:, :] = jnp.broadcast_to(lp[...], (SENT - BLOCK, WIDTH))
    pl.semaphore_wait(barrier, len(peers))

    copies = {}

    def send(key, src, dst, dev):
        copy = pltpu.make_async_remote_copy(
            src_ref=src, dst_ref=dst, send_sem=send_sem.at[SEM[key]], recv_sem=recv_sem.at[SEM[key]],
            device_id=dev, device_id_type=MESH,
        )
        copy.start()
        copies[key] = copy

    def got(key):
        copies[key].wait_recv()

    def send_p(src, dst, dev):
        send(("p", dst), pb.at[src], pb.at[dst], dev)

    def send_a(src, dst, dev):
        send(("a", dst), ab.at[src], ab.at[dst], dev)

    def got_p(j, dy, kk):
        got(("p", ps(j, dy, kk)))

    def got_a(dz, dx):
        got(("a", as_(dz, dx)))

    def a_along_x(dz):
        for d in (1, -1, 2):
            send_a(as_(dz, 0), as_(dz, -d), x_dev[d % NUM_X])

    def p_along_y(ds):
        for d in ds:
            send_p(ps(0, 0, 0), ps(0, -d, 0), y_dev[d % NUM_Y])

    def to_sibling(j, dy):
        send_p(ps(j, dy, 0), ps(j, dy, 1), sibling)

    def to_pair(dy):
        send_p(ps(0, dy, 0), ps(1, dy, 0), z_pair)

    def spread(dy):
        got_p(0, dy, 0)
        to_pair(dy)
        to_sibling(0, dy)

    def from_pair(dy):
        got_p(1, dy, 0)
        to_sibling(1, dy)

    def onward():
        for s in (1, -1):
            got_p(0, -2 * s, 0)
            send_p(ps(0, -2 * s, 0), ps(0, -3 * s, 0), y_dev[s % NUM_Y])
        source = jnp.where(core == 0, ps(0, -2, 0), ps(0, 2, 0))
        send_p(source, ps(0, 4, 0), row_dev(zl, (y + jnp.where(core == 0, 2, 6)) % NUM_Y, core))
        for s in (1, -1):
            to_pair(-2 * s)
            to_sibling(0, -2 * s)

    def prepare_a(dz):
        first, count = a_slots(dz)
        for i in range(first, first + count):
            rows = slice(i * BLOCK, (i + 1) * BLOCK)
            at[:, rows] = ab[i, :BLOCK, :].T
            lse = ab[i, BLOCK:, :].astype(f32)[0:1, :]
            ub[rows, :] = jnp.broadcast_to(jnp.exp(TOP - lse), (BLOCK, BLOCK)).T

    def prepare_p(name):
        first, count = p_slots(name)
        for i in range(first, first + count):
            lse = pb[i, BLOCK:, :].astype(f32)[0:8, :]
            vb[:, i * BLOCK:(i + 1) * BLOCK] = jnp.exp(TOP - lse)

    touched = set()

    def tile(row_slots, col_slots):
        (r0, nr), (c0, nc) = row_slots, col_slots
        rows, cols = slice(r0 * BLOCK, (r0 + nr) * BLOCK), slice(c0 * BLOCK, (c0 + nc) * BLOCK)
        a = ab[r0:r0 + nr, :BLOCK, :].reshape(nr * BLOCK, WIDTH)
        p = pb[c0:c0 + nc, :BLOCK, :].reshape(nc * BLOCK, WIDTH)
        t = lax.dot_general(a, p, (((1,), (1,)), ((), ())), preferred_element_type=f32)
        weight = jnp.concatenate([ub[rows, :]] * nc, axis=1) + vb[0:1, cols]
        soft = (jnp.exp2(t * SCALE - TOP * LOG2E) * weight).astype(bf16)
        to_rows = jnp.dot(soft, p, preferred_element_type=f32)
        to_cols = jnp.dot(at[:, rows], soft, preferred_element_type=f32)
        row_keys = {("a", i) for i in range(r0, r0 + nr)}
        col_keys = {("p", i) for i in range(c0, c0 + nc)}
        if row_keys <= touched:
            acc_a[rows, :] += to_rows
        else:
            assert not row_keys & touched
            acc_a[rows, :] = to_rows
        if col_keys <= touched:
            acc_p[:, cols] += to_cols
        else:
            assert not col_keys & touched
            acc_p[:, cols] = to_cols
        touched.update(row_keys | col_keys)

    def own_a(dz, dx):
        i = as_(dz, dx)
        return acc_a[i * BLOCK:(i + 1) * BLOCK, :]

    def own_p(j, dy, kk):
        i = ps(j, dy, kk)
        return acc_p[:, i * BLOCK:(i + 1) * BLOCK]

    def send_sum(key, value, dev):
        i = SUM_SLOT[key]
        out_s[i] = value.astype(bf16)
        send(key, out_s.at[i], in_s.at[i], dev)

    def arrived(*key):
        got(key)
        return in_s[SUM_SLOT[key]].astype(f32)

    def core_sums(*names):
        for name in names:
            for j, dy in P_GROUPS[name]:
                send_sum(("core", j, dy % NUM_Y), own_p(j, dy, 1), sibling)

    def chip_sum(j, dy):
        return own_p(j, dy, 0) + arrived("core", j, dy % NUM_Y)

    def z_sums(*names):
        for name in names:
            for j, dy in P_GROUPS[name]:
                if j == 1:
                    send_sum(("z", dy % NUM_Y), chip_sum(1, dy), z_pair)

    def pair_far_sums():
        for j, dy in P_GROUPS["pair_far"]:
            send_sum(("pair", dy % NUM_Y), chip_sum(j, dy), pair_dev[dy % NUM_Y])

    def pair_sum(dy):
        if dy in (3, -3, 4):
            return chip_sum(0, dy)
        return chip_sum(0, dy) + arrived("z", dy % NUM_Y)

    def y_sums(name):
        for _, dy in P_GROUPS[name]:
            send_sum(("y", dy % NUM_Y), pair_sum(dy), y_dev[dy % NUM_Y])

    def x_sums(dz):
        for dx in (2, 1, -1):
            send_sum(("x", dz % NUM_ZH, dx % NUM_X), own_a(dz, dx), x_dev[dx % NUM_X])

    def x_total(dz):
        total = own_a(dz, 0)
        for dx in range(1, NUM_X):
            total += arrived("x", dz % NUM_ZH, dx)
        return total

    def zh_sum(dz):
        send_sum(("zh", dz % NUM_ZH), x_total(dz), zh_dev[dz % NUM_ZH])

    def diagonal(*names):
        for name in names:
            for j, dy in P_GROUPS[name]:

                @pl.when((c == r // 2) & ((core + zl) % 2 == j))
                def _():
                    for kk in (0, 1):
                        k = ps(j, dy, kk)
                        other = (y + dy + NUM_Y) % NUM_Y * 2 + (core + kk) % 2
                        dz, dx = (other // NUM_X + NUM_ZH - zh) % NUM_ZH, (other % NUM_X + NUM_X - x) % NUM_X
                        i = NUM_X * jnp.where(dz <= 1, 2 * dz, 7 - 2 * dz) + jnp.where(dx <= 1, 2 * dx, 7 - 2 * dx)
                        rows = pl.ds(pl.multiple_of(i * BLOCK, BLOCK), BLOCK)
                        cols = slice(k * BLOCK, (k + 1) * BLOCK)
                        acc_a[rows, :] -= 2.0 * pb[k, :BLOCK, :].astype(f32)
                        acc_p[:, cols] -= 2.0 * at[:, rows].astype(f32)

    def sums_of(*names):
        diagonal(*names)
        core_sums(*names)

    send_a(as_(0, 0), as_(-1, 0), zh_dev[1])
    send_a(as_(0, 0), as_(1, 0), zh_dev[3])
    p_along_y((2, -2, 1, -1))
    to_pair(0)
    a_along_x(0)
    to_sibling(0, 0)

    for s in (1, -1):
        spread(s)
    from_pair(0)
    got_a(-1, 0)
    send_a(as_(-1, 0), as_(2, 0), zh_dev[1])
    a_along_x(-1)
    got_a(1, 0)
    a_along_x(1)
    onward()
    for d in (1, -1, 2):
        got_a(0, d)
    prepare_a(0)
    for s in (1, -1):
        got_p(0, s, 1)
    prepare_p("near")
    tile(a_slots(0), p_slots("near"))
    for s in (1, -1):
        got_p(0, 2 * s, 1)
    prepare_p("next")
    tile(a_slots(0), p_slots("next"))
    for s in (1, -1):
        from_pair(s)
    got_a(2, 0)
    a_along_x(2)
    for d in (1, -1, 2):
        got_a(-1, d)
    prepare_a(-1)
    tile(a_slots(-1), p_slots("near", "next"))
    for s in (1, -1):
        from_pair(2 * s)
    for d in (3, -3, 4):
        spread(d)
    for d in (1, -1, 2):
        got_a(1, d)
    prepare_a(1)
    tile(a_slots(1), p_slots("near", "next"))
    for s in (1, -1):
        got_p(1, s, 1)
    prepare_p("pair_near")
    tile(a_slots(0, -1, 1), p_slots("pair_near"))
    for d in (3, -3, 4):
        from_pair(d)
    for d in (1, -1, 2):
        got_a(2, d)
    prepare_a(2)
    tile(a_slots(2), p_slots("near", "next", "pair_near"))
    sums_of("pair_near", "next", "near")

    for s in (1, -1):
        got_p(1, 2 * s, 1)
    prepare_p("pair_next")
    tile(a_slots(0, -1, 1, 2), p_slots("pair_next"))
    sums_of("pair_next")
    z_sums("pair_near")
    for d in (3, -3, 4):
        got_p(1, d, 1)
    prepare_p("pair_far")
    tile(a_slots(0, -1, 1, 2), p_slots("pair_far"))
    sums_of("pair_far")
    z_sums("pair_next")
    for d in (3, -3, 4):
        got_p(0, d, 1)
    prepare_p("far")
    got_p(0, 0, 1)
    got_p(1, 0, 1)
    prepare_p("home")
    tile(a_slots(2), p_slots("far"))
    tile(a_slots(2), p_slots("home"))
    diagonal("far", "home")
    x_sums(2)
    y_sums("near")
    pair_far_sums()
    tile(a_slots(-1), p_slots("far"))
    tile(a_slots(-1), p_slots("home"))
    x_sums(-1)
    tile(a_slots(1), p_slots("far"))
    tile(a_slots(1), p_slots("home"))
    x_sums(1)
    y_sums("next")
    tile(a_slots(0), p_slots("far"))
    core_sums("far")
    tile(a_slots(0), p_slots("home"))
    core_sums("home")
    x_sums(0)
    y_sums("far")
    z_sums("home")
    zh_sum(2)
    zh_sum(-1)
    zh_sum(1)
    total_p = pair_sum(0)
    for dy in (1, -1, 2, -2, 3, -3, 4):
        total_p += arrived("y", dy % NUM_Y)
    for dy in (3, -3, 4):
        total_p += arrived("pair", dy % NUM_Y)
    dp_out[...] = 5.0 * total_p.T
    total_a = x_total(0)
    for dz in (2, 3, 1):
        total_a += arrived("zh", dz)
    da_out[...] = 5.0 * total_a
    for copy in copies.values():
        copy.wait_send()


def on_device(anchors, positives, row_lse, column_logsumexp):
    vmem = pl.BlockSpec(memory_space=pltpu.VMEM)
    anywhere = pl.BlockSpec(memory_space=pltpu.HBM)
    block = jax.ShapeDtypeStruct((BLOCK, WIDTH), f32)
    return pl.pallas_call(
        kernel,
        out_shape=(block, block),
        in_specs=[anywhere] * 4,
        out_specs=(vmem, vmem),
        scratch_shapes=[
            pltpu.VMEM((ROWS, SENT, WIDTH), bf16),
            pltpu.VMEM((COLUMNS, SENT, WIDTH), bf16),
            pltpu.VMEM((WIDTH, ROWS * BLOCK), bf16),
            pltpu.VMEM((ROWS * BLOCK, BLOCK), f32),
            pltpu.VMEM((8, COLUMNS * BLOCK), f32),
            pltpu.VMEM((ROWS * BLOCK, WIDTH), f32),
            pltpu.VMEM((WIDTH, COLUMNS * BLOCK), f32),
            pltpu.VMEM((len(SUM_KEYS), BLOCK, WIDTH), bf16),
            pltpu.VMEM((len(SUM_KEYS), BLOCK, WIDTH), bf16),
            pltpu.VMEM((1, BLOCK), bf16),
            pltpu.VMEM((1, BLOCK), bf16),
            pltpu.SemaphoreType.DMA((len(SEM),)),
            pltpu.SemaphoreType.DMA((len(SEM),)),
            pltpu.SemaphoreType.DMA((4,)),
        ],
        compiler_params=pltpu.CompilerParams(
            collective_id=0, has_side_effects=True, vmem_limit_bytes=48 * 2**20
        ),
        name="infonce_backward",
    )(*(
        pltpu.with_memory_space_constraint(value, pltpu.HBM)
        for value in (anchors, positives, row_lse.reshape(1, BLOCK), column_logsumexp.reshape(1, BLOCK))
    ))


def solution(mesh):
    return jax.shard_map(
        on_device,
        mesh=mesh,
        in_specs=(
            P(("row", "col"), None),
            P(("col", "row"), None),
            P(("row", "col")),
            P(("col", "row")),
        ),
        out_specs=(P(("row", "col"), None), P(("col", "row"), None)),
        check_vma=False,
    )
```
